256 devices in a mesh: dom: 32 (over z, y), rep: 8 (over x, core).
Axes of the slice: x: 4, y: 4, z: 8, core: 2. Of those that a mesh axis runs over, the one named last changes fastest.
Arguments:
- features: bfloat16 [131072, 256], P(('dom', 'rep')), may hold values from -6 to 6
- cotangent: bfloat16 [131072, 256], P(('dom', 'rep')), may hold values from -6 to 6
- w_self: bfloat16 [256, 256], replicated, may hold values from -0.375 to 0.375
- w_neigh: bfloat16 [256, 256], replicated, may hold values from -0.375 to 0.375
- tile_values: bfloat16 [32, 8, 256, 128, 128], P('dom', 'rep'), may hold values from -0.109375 to 0.109375
- tile_rows: int32 [32, 8, 256], P('dom', 'rep'), may hold values from 0 to 31
- tile_sources: int32 [32, 8, 256], P('dom', 'rep'), may hold values from 0 to 31
- tile_counts: int32 [32, 8], P('dom', 'rep'), may hold values from 32 to 256, as said below
- needed: int32 [32, 8, 32], replicated, may hold values from 0 to 3
Outputs:
- output: bfloat16 [131072, 256], P(('dom', 'rep'))
- grad_features: bfloat16 [131072, 256], P(('dom', 'rep'))
- grad_w_self: float32 [256, 256], replicated
- grad_w_neigh: float32 [256, 256], replicated
The draws below stay inside these ranges and needn't reach their ends.
Inputs may be any that keep to these rules, and one draw needn't show every extreme that they name: Slots from tile_counts on are not part of the adjacency. In every draw some devices use all 256 slots.
All inputs are finite; a program needn't handle non-finite values.
Results may differ from the reference program's by a relative error of at most 0.022.
Values may be sent and summed in bfloat16 or wider, within the bound.
No kernel may reach another device: no remote copies, remote signals or barrier semaphores. Data moves between devices by JAX's collectives and lax.ppermute only.
A program may use at most 128 MiB of HBM per device.

```python
import math
import jax
import jax.numpy as jnp
from jax import lax

F = 256
TILE = 128
SR = 512
K = 256
PARTS_SIZE = 32
REPS = 8
NODES = 131072
CT = 4
RT = 32


def draw_tile_counts(key, part):
    key = jax.random.fold_in(key, 11)
    first, second = jax.random.split(key)
    drawn = jax.random.randint(first, (PARTS_SIZE * REPS,), K // 8, K // 2 + 1)
    chosen = jax.random.permutation(second, PARTS_SIZE * REPS)[:8]
    drawn = drawn.at[chosen].set(K)
    return drawn.reshape(PARTS_SIZE, REPS).astype(jnp.int32)


def touch_ends(values, rng, smallest, largest):
    shape = values.shape
    spot = [jax.random.randint(jax.random.fold_in(rng, axis), (), 0, shape[axis]) for axis in range(len(shape))]
    values = values.at[tuple(spot)].set(smallest)
    longest = shape.index(max(shape))
    spot[longest] = (spot[longest] + 1) % shape[longest]
    return values.at[tuple(spot)].set(largest)


def level_of(stream_key, extent, shards, least, high):
    def one(dim, parts):
        steps = jax.random.uniform(jax.random.fold_in(jax.random.fold_in(stream_key, 6), dim), (parts,), jnp.float32, least / len(shards), high / len(shards))
        return jnp.repeat(jnp.exp(steps), extent[dim] // parts).reshape((-1,) + (1,) * (len(extent) - dim - 1))

    gain = one(*shards[0])
    for cut in shards[1:]:
        gain = gain * one(*cut)
    return gain


def scatter_about(key, extent, scale, bound, cuts=(), kind=jnp.bfloat16):
    entries = scale * jax.random.normal(key, extent, jnp.float32)
    if cuts:
        entries = entries * level_of(key, extent, cuts, -0.22, 0.18)
    return jnp.clip(entries, -bound, bound).astype(kind)


def setup_inputs(seed: int = 0) -> dict:
    arg_keys = jax.random.split(jax.random.key(seed), 10)
    return {
        "features": scatter_about(arg_keys[0], (NODES, F), 1.0, 6.0, ((0, 256),)),
        "cotangent": scatter_about(arg_keys[1], (NODES, F), 1.0, 6.0, ((0, 256),)),
        "w_self": scatter_about(arg_keys[2], (F, F), F ** -0.5, 0.375),
        "w_neigh": scatter_about(arg_keys[3], (F, F), F ** -0.5, 0.375),
        "tile_values": scatter_about(arg_keys[4], (PARTS_SIZE, REPS, K, TILE, TILE), (3 * K * TILE * TILE // (8 * SR)) ** -0.5, 0.109375, ((0, 32), (1, 8))),
        "tile_rows": touch_ends(jax.random.randint(arg_keys[5], (PARTS_SIZE, REPS, K), 0, RT), jax.random.fold_in(arg_keys[5], 1), 0, RT - 1).astype(jnp.int32),
        "tile_sources": touch_ends(jax.random.randint(arg_keys[6], (PARTS_SIZE, REPS, K), 0, PARTS_SIZE), jax.random.fold_in(arg_keys[6], 1), 0, PARTS_SIZE - 1).astype(jnp.int32),
        "tile_counts": draw_tile_counts(jax.random.fold_in(arg_keys[9], 71), 0),
        "needed": touch_ends(jax.random.randint(arg_keys[8], (PARTS_SIZE, REPS, PARTS_SIZE), 0, CT), jax.random.fold_in(arg_keys[8], 1), 0, CT - 1).astype(jnp.int32),
    }


def reference(features, cotangent, w_self, w_neigh, tile_values, tile_rows, tile_sources, tile_counts, needed):
    blocks = features.reshape(PARTS_SIZE, REPS, CT, TILE, F)
    slots = jnp.arange(K)

    def masked_values(p, r):
        inside = slots < tile_counts[p, r]
        return jnp.where(inside[:, None, None], tile_values[p, r].astype(jnp.float32), jnp.zeros((), jnp.float32))

    def forward_one(running, index):
        p = index // REPS
        r = index % REPS
        columns = blocks[jnp.arange(PARTS_SIZE), r, needed[p, r]].astype(jnp.float32)
        picked = columns[tile_sources[p, r]]
        product = jnp.einsum('kij,kjf->kif', masked_values(p, r), picked)
        local = jnp.zeros((RT, TILE, F), jnp.float32).at[tile_rows[p, r]].add(product)
        return (running.at[p].add(local), None)
    start = jnp.zeros((PARTS_SIZE, RT, TILE, F), jnp.float32)
    summed, _ = lax.scan(forward_one, start, jnp.arange(PARTS_SIZE * REPS, dtype=jnp.int32))
    aggregate = summed.reshape(NODES, F).astype(jnp.bfloat16)
    pre_act = jnp.dot(features, w_self, preferred_element_type=jnp.float32) + jnp.dot(aggregate, w_neigh, preferred_element_type=jnp.float32)
    logistic = jax.nn.sigmoid(pre_act)
    output = (pre_act * logistic).astype(jnp.bfloat16)
    derivative = logistic * (1.0 + pre_act * (1.0 - logistic))
    grad_pre = (cotangent.astype(jnp.float32) * derivative).astype(jnp.bfloat16)
    grad_agg = jnp.dot(grad_pre, w_neigh.T, preferred_element_type=jnp.float32).astype(jnp.bfloat16)
    grad_scale = 1.0 / math.sqrt(NODES)
    grad_w_self = jnp.dot(features.T, grad_pre, preferred_element_type=jnp.float32) * grad_scale
    grad_w_neigh = jnp.dot(aggregate.T, grad_pre, preferred_element_type=jnp.float32) * grad_scale
    grad_tiles = grad_agg.reshape(PARTS_SIZE, RT, TILE, F)

    def backward_one(running, index):
        p = index // REPS
        r = index % REPS
        picked = grad_tiles[p].astype(jnp.float32)[tile_rows[p, r]]
        contrib = jnp.einsum('kji,kjf->kif', masked_values(p, r), picked)
        local = jnp.zeros((PARTS_SIZE, TILE, F), jnp.float32).at[tile_sources[p, r]].add(contrib)
        local = lax.optimization_barrier(local.astype(jnp.bfloat16)).astype(jnp.float32)
        return (running.at[jnp.arange(PARTS_SIZE), r, needed[p, r]].add(local), None)
    begin = jnp.zeros((PARTS_SIZE, REPS, CT, TILE, F), jnp.float32)
    returned, _ = lax.scan(backward_one, begin, jnp.arange(PARTS_SIZE * REPS, dtype=jnp.int32))
    self_grad = jnp.dot(grad_pre, w_self.T, preferred_element_type=jnp.float32)
    grad_features = (self_grad + returned.reshape(NODES, F)).astype(jnp.bfloat16)
    return (output, grad_features, grad_w_self, grad_w_neigh)
```

```python
import functools
import math

import jax
import jax.numpy as jnp
from jax import lax
from jax.experimental import pallas as pl
from jax.experimental.pallas import tpu as pltpu
from jax.sharding import Mesh
from jax.sharding import PartitionSpec as P

F32 = jnp.float32
BF16 = jnp.bfloat16
BLOCK = 32
UNROLL = 16
VMEM_LIMIT = 40 * 2**20
AXES = ("z", "y", "x", "c")
SIZES = (8, 4, 4, 2)
DOM = ("z", "y")
REP = ("x", "c")


def select_kernel(index, blocks, out, sems):
    copies = [
        pltpu.make_async_copy(blocks.at[index[i]], out.at[i], sems.at[i])
        for i in range(out.shape[0])
    ]
    for copy in copies:
        copy.start()
    for copy in copies:
        copy.wait()


def select(index, blocks):
    count = index.shape[0]
    return pl.pallas_call(
        select_kernel,
        out_shape=jax.ShapeDtypeStruct((count,) + blocks.shape[1:], blocks.dtype),
        grid_spec=pltpu.PrefetchScalarGridSpec(
            num_scalar_prefetch=1,
            grid=(),
            in_specs=[pl.BlockSpec(memory_space=pl.ANY)],
            out_specs=pl.BlockSpec(memory_space=pl.ANY),
            scratch_shapes=[pltpu.SemaphoreType.DMA((count,))],
        ),
        name="select",
    )(index, blocks)


def accumulate_slots(step, used, add_slot):
    def group(g, carry):
        for u in range(UNROLL):
            k = g * UNROLL + u
            add_slot(k, step * BLOCK + k, step * BLOCK + k < used)
        return carry

    left = jnp.clip(used - step * BLOCK, 0, BLOCK)
    lax.fori_loop(0, (left + UNROLL - 1) // UNROLL, group, 0)


def forward_kernel(rows, sources, info, values, columns, keep, send, total):
    step = pl.program_id(0)
    used = info[0]
    core = info[1]

    @pl.when(step == 0)
    def _():
        total[...] = jnp.zeros_like(total)

    def add_slot(k, slot, inside):
        row = jnp.where(inside, rows[slot], 32)
        source = sources[slot]
        place = (source % 4) * 8 + source // 4
        total[row] += jnp.dot(values[k], columns[place], preferred_element_type=F32)

    accumulate_slots(step, used, add_slot)

    @pl.when(step == pl.num_programs(0) - 1)
    def _():
        for x in range(4):
            keep[x] = total[pl.ds(x * 8 + core * 4, 4)].astype(BF16)
            send[x] = total[pl.ds(x * 8 + (1 - core) * 4, 4)].astype(BF16)


def backward_kernel(rows, sources, info, values, grads, out, total):
    step = pl.program_id(0)
    used = info[0]

    @pl.when(step == 0)
    def _():
        total[...] = jnp.zeros_like(total)

    def add_slot(k, slot, inside):
        source = jnp.where(inside, sources[slot], 32)
        total[source] += lax.dot_general(
            values[k], grads[rows[slot]], (((0,), (0,)), ((), ())), preferred_element_type=F32
        )

    accumulate_slots(step, used, add_slot)

    @pl.when(step == pl.num_programs(0) - 1)
    def _():
        out[...] = total[:32].astype(BF16)


def over_slots(kernel, name, out_shapes, rows, sources, info, values, operand):
    slots = values.shape[0]

    def values_at(step, rows, sources, info):
        return (jnp.minimum(step, (info[0] - 1) // BLOCK), 0, 0)

    def whole(shape):
        return pl.BlockSpec(shape, lambda *_: (0,) * len(shape))

    return pl.pallas_call(
        kernel,
        out_shape=[jax.ShapeDtypeStruct(shape, BF16) for shape in out_shapes],
        grid_spec=pltpu.PrefetchScalarGridSpec(
            num_scalar_prefetch=3,
            grid=(slots // BLOCK,),
            in_specs=[pl.BlockSpec((BLOCK, 128, 128), values_at), whole(operand.shape)],
            out_specs=[whole(shape) for shape in out_shapes],
            scratch_shapes=[pltpu.VMEM((33, 128, 256), F32)],
        ),
        compiler_params=pltpu.CompilerParams(vmem_limit_bytes=VMEM_LIMIT),
        cost_estimate=pl.CostEstimate(
            flops=2 * slots * 128 * 128 * 256, bytes_accessed=slots * 32768 + 2**22, transcendentals=0
        ),
        name=name,
    )(rows, sources, info, values, operand)


def dense_kernel(features, cotangent, w_self, w_neigh, parts, output, grad_pre, grad_agg, aggregate):
    summed = parts[0].astype(F32)
    for x in range(1, 4):
        summed += parts[x].astype(F32)
    agg = summed.astype(BF16)
    aggregate[...] = agg
    pre = jnp.dot(features[...], w_self[...], preferred_element_type=F32)
    pre += jnp.dot(agg, w_neigh[...], preferred_element_type=F32)
    logistic = jax.nn.sigmoid(pre)
    output[...] = (pre * logistic).astype(BF16)
    derivative = logistic * (1.0 + pre * (1.0 - logistic))
    grad = (cotangent[...].astype(F32) * derivative).astype(BF16)
    grad_pre[...] = grad
    grad_agg[...] = lax.dot_general(
        grad, w_neigh[...], (((1,), (1,)), ((), ())), preferred_element_type=F32
    ).astype(BF16)


def dense(features, cotangent, w_self, w_neigh, parts):
    shape = jax.ShapeDtypeStruct(features.shape, BF16)
    return pl.pallas_call(
        dense_kernel,
        out_shape=[shape] * 4,
        compiler_params=pltpu.CompilerParams(vmem_limit_bytes=VMEM_LIMIT),
        name="dense",
    )(features, cotangent, w_self, w_neigh, parts)


def final_kernel(index, self_grad, returned, out, total):
    step = pl.program_id(0)
    count = returned.shape[0]

    @pl.when(step == 0)
    def _():
        total[...] = self_grad[...]

    for i in range(count):
        total[index[step * count + i]] += returned[i].astype(F32)

    @pl.when(step == pl.num_programs(0) - 1)
    def _():
        out[...] = total[...].astype(BF16)


def final(index, self_grad, returned):
    shape = self_grad.shape
    return pl.pallas_call(
        final_kernel,
        out_shape=jax.ShapeDtypeStruct(shape, BF16),
        grid_spec=pltpu.PrefetchScalarGridSpec(
            num_scalar_prefetch=1,
            grid=(4,),
            in_specs=[
                pl.BlockSpec(shape, lambda *_: (0, 0, 0)),
                pl.BlockSpec((8, 128, 256), lambda i, _: (i, 0, 0)),
            ],
            out_specs=pl.BlockSpec(shape, lambda *_: (0, 0, 0)),
            scratch_shapes=[pltpu.VMEM(shape, F32)],
        ),
        name="final",
    )(index, self_grad, returned)


def body(
    features, cotangent, w_self, w_neigh, tile_values, tile_rows, tile_sources, tile_counts, needed
):
    z, y, x, c = (lax.axis_index(a) for a in AXES)
    rank = x * 2 + c
    values = tile_values[0, 0]
    rows = tile_rows[0, 0]
    sources = tile_sources[0, 0]
    info = jnp.stack([tile_counts[0, 0], c.astype(jnp.int32)])
    shape = (4, 128, 256)

    with jax.named_scope("gather_columns"):
        wanted = needed.reshape(8, 4, 8, 8, 4)
        asked = lax.dynamic_slice(wanted, (z, 0, rank, 0, y), (1, 4, 1, 8, 1)).reshape(4, 8)
        asked = (asked + 4 * jnp.arange(8)[None, :]).reshape(32)
        column_blocks = lax.all_gather(features.reshape(shape), "z", axis=0, tiled=True)
        columns = lax.all_to_all(select(asked, column_blocks), "y", 0, 0, tiled=True)

    with jax.named_scope("aggregate"):
        kept, sent = over_slots(
            forward_kernel, "forward", [(4,) + shape] * 2, rows, sources, info, values, columns
        )
        other = lax.ppermute(sent, "c", [(0, 1), (1, 0)])
        pair = (kept.astype(F32) + other.astype(F32)).astype(BF16)
        parts = lax.all_to_all(pair, "x", 0, 0, tiled=True)

    with jax.named_scope("dense"):
        output, grad_pre, grad_agg, aggregate = dense(
            features, cotangent, w_self, w_neigh, parts.reshape(4, 512, 256)
        )

    with jax.named_scope("backward"):
        grads = lax.all_gather(grad_agg.reshape(shape), REP, axis=0, tiled=True)
        (neighbour,) = over_slots(
            backward_kernel, "backward", [(32, 128, 256)], rows, sources, info, values, grads
        )
        returned = lax.all_to_all(neighbour, DOM, 0, 0, tiled=True)

    with jax.named_scope("weights"):
        local = jnp.concatenate(
            [
                lax.dot_general(a, grad_pre, (((0,), (0,)), ((), ())), preferred_element_type=F32)
                for a in (features, aggregate)
            ]
        )
        share = lax.all_to_all(local.reshape(8, 64, 256), REP, 0, 0, tiled=True).sum(0)
        share = lax.all_gather(share, "y", axis=0, tiled=False).sum(0)
        share = lax.all_gather(share, "z", axis=0, tiled=False).sum(0)
        share = share * (1.0 / math.sqrt(512 * 256))
        grad_w = lax.all_gather(share, REP, axis=0, tiled=True)

    with jax.named_scope("final"):
        self_grad = lax.dot_general(
            grad_pre, w_self, (((1,), (1,)), ((), ())), preferred_element_type=F32
        )
        mine = lax.dynamic_slice(needed, (0, rank, z * 4 + y), (32, 1, 1)).reshape(32)
        grad_features = final(mine, self_grad.reshape(shape), returned)

    return (output, grad_features.reshape(512, 256), grad_w[:256], grad_w[256:])


def solution(mesh):
    chips = Mesh(mesh.devices.reshape(SIZES), AXES)
    nodes = P(AXES, None)
    in_specs = (
        nodes,
        nodes,
        P(),
        P(),
        P(DOM, REP, None, None, None),
        P(DOM, REP, None),
        P(DOM, REP, None),
        P(DOM, REP),
        P(),
    )
    out_specs = (nodes, nodes, P(), P())
    return jax.shard_map(body, mesh=chips, in_specs=in_specs, out_specs=out_specs, check_vma=False)
```

```python
import functools
import math

import jax
import jax.numpy as jnp
from jax import lax
from jax.experimental import pallas as pl
from jax.experimental.pallas import tpu as pltpu
from jax.sharding import Mesh
from jax.sharding import PartitionSpec as P

F32 = jnp.float32
BF16 = jnp.bfloat16
PARTS = 2
WIDTH = 256 // PARTS
BLOCK = 16
VMEM_LIMIT = 54 * 2**20
AXES = ("z", "y", "x", "c")
SIZES = (8, 4, 4, 2)
DOM = ("z", "y")
REP = ("x", "c")


def select_kernel(index, blocks, out):
    for i in range(out.shape[0]):
        out[i] = blocks[index[i]]


def select(index, blocks):
    return pl.pallas_call(
        select_kernel,
        out_shape=jax.ShapeDtypeStruct((index.shape[0],) + blocks.shape[1:], blocks.dtype),
        grid_spec=pltpu.PrefetchScalarGridSpec(
            num_scalar_prefetch=1,
            grid=(),
            in_specs=[pl.BlockSpec(memory_space=pltpu.VMEM)],
            out_specs=pl.BlockSpec(memory_space=pltpu.VMEM),
        ),
        compiler_params=pltpu.CompilerParams(vmem_limit_bytes=8 * 2**20),
        name="select",
    )(index, blocks)


def copies_of(source, target, size, sems):
    rows = pl.ds(0, target.shape[1])
    return [
        pltpu.make_async_copy(
            source.at[pl.ds(i * size, size), rows], target.at[pl.ds(i * size, size)], sems.at[i]
        )
        for i in range(source.shape[0] // size)
    ]


def accumulate_slots(used, values, tiles, total, sems, piece_copies, add_slot):
    for copy in piece_copies:
        copy.start()
    for copy in copies_of(values, tiles, BLOCK, sems):
        copy.start()
    total[...] = jnp.zeros_like(total)
    for copy in piece_copies:
        copy.wait()

    def block(b, carry):
        first = b * BLOCK
        pltpu.make_async_copy(
            values.at[pl.ds(first, BLOCK)], tiles.at[pl.ds(first, BLOCK)], sems.at[b]
        ).wait()

        @pl.when(first < used)
        def _():
            for u in range(BLOCK):
                add_slot(first + u)

        return carry

    lax.fori_loop(0, values.shape[0] // BLOCK, block, 0)


def forward_kernel(targets, places, info, values, columns, keep, send, tiles, total, sems):
    used, x, core = info[0], info[1], info[2]

    def add_slot(k):
        total[targets[k]] += jnp.dot(tiles[k], columns[places[k]], preferred_element_type=F32)

    accumulate_slots(used, values, tiles, total, sems, [], add_slot)
    for k in range(4):
        chip = lax.rem(x + k, 4) * 8
        keep[k] = total[pl.ds(chip + core * 4, 4)].astype(BF16)
        send[k] = total[pl.ds(chip + (1 - core) * 4, 4)].astype(BF16)


def backward_kernel(targets, places, info, values, *refs):
    pieces, (out, tiles, total, sems, held, piece_sems) = refs[:8], refs[-6:]

    def add_slot(k):
        total[targets[k]] += jnp.dot(held[places[k]], tiles[k], preferred_element_type=F32)

    piece_copies = [
        pltpu.make_async_copy(piece, held.at[pl.ds(i * 4, 4)], piece_sems.at[i])
        for i, piece in enumerate(pieces)
    ]
    accumulate_slots(info[0], values, tiles, total, sems, piece_copies, add_slot)
    out[:, :WIDTH, :] = total[:32].astype(BF16)
    for share in refs[8:-6]:
        for i in range(32):
            out[i, WIDTH:, :] = share[...]


def over_slots(kernel, name, out_shapes, targets, places, info, values, pieces, extra=()):
    slots = values.shape[0]
    tile = pieces[0].shape[1:]
    scratch = [
        pltpu.VMEM(values.shape, BF16),
        pltpu.VMEM((33,) + tile, F32),
        pltpu.SemaphoreType.DMA((slots // BLOCK,)),
    ]
    if len(pieces) > 1:
        scratch += [
            pltpu.VMEM((32,) + tile, BF16),
            pltpu.SemaphoreType.DMA((len(pieces),)),
        ]
    piece_space = pl.ANY if len(pieces) > 1 else pltpu.VMEM
    return pl.pallas_call(
        kernel,
        out_shape=[jax.ShapeDtypeStruct(shape, BF16) for shape in out_shapes],
        grid_spec=pltpu.PrefetchScalarGridSpec(
            num_scalar_prefetch=3,
            grid=(),
            in_specs=[pl.BlockSpec(memory_space=pltpu.HBM)]
            + [pl.BlockSpec(memory_space=piece_space)] * len(pieces)
            + [pl.BlockSpec(memory_space=pltpu.VMEM)] * len(extra),
            out_specs=[pl.BlockSpec(memory_space=pltpu.VMEM)] * len(out_shapes),
            scratch_shapes=scratch,
        ),
        compiler_params=pltpu.CompilerParams(vmem_limit_bytes=VMEM_LIMIT),
        cost_estimate=pl.CostEstimate(
            flops=2 * slots * 128 * 128 * 256, bytes_accessed=slots * 32768 + 2**22, transcendentals=0
        ),
        name=name,
    )(targets, places, info, values, *pieces, *extra)


def dense_kernel(features, cotangent, w_self, w_neigh, *refs):
    sums, refs = refs[:4], refs[4:]
    output, grad_pre, grad_aggs, local_weights = refs[0], refs[1], refs[2 : 2 + PARTS], refs[2 + PARTS]
    summed = sums[0][...].astype(F32)
    for part in sums[1:]:
        summed += part[...].astype(F32)
    agg = summed.astype(BF16)
    pre = jnp.dot(features[...], w_self[...], preferred_element_type=F32)
    pre += jnp.dot(agg, w_neigh[...], preferred_element_type=F32)
    logistic = jax.nn.sigmoid(pre)
    output[...] = (pre * logistic).astype(BF16)
    derivative = logistic * (1.0 + pre * (1.0 - logistic))
    grad = (cotangent[...].astype(F32) * derivative).astype(BF16)
    grad_pre[...] = grad
    for h in range(PARTS):
        turned = lax.dot_general(
            w_neigh[h * WIDTH : (h + 1) * WIDTH, :],
            grad,
            (((1,), (1,)), ((), ())),
            preferred_element_type=F32,
        ).astype(BF16)
        for t in range(4):
            grad_aggs[h][t] = turned[:, t * 128 : (t + 1) * 128]
    for i, left in enumerate((features[...], agg)):
        product = lax.dot_general(left, grad, (((0,), (0,)), ((), ())), preferred_element_type=F32)
        local_weights[i * 256 : (i + 1) * 256, :] = product.astype(BF16)


def dense(features, cotangent, w_self, w_neigh, sums):
    whole = jax.ShapeDtypeStruct(features.shape, BF16)
    part = jax.ShapeDtypeStruct((4, WIDTH, 128), BF16)
    return pl.pallas_call(
        dense_kernel,
        out_shape=[whole, whole] + [part] * PARTS + [whole],
        compiler_params=pltpu.CompilerParams(vmem_limit_bytes=16 * 2**20),
        name="dense",
    )(features, cotangent, w_self, w_neigh, *sums)


def place_kernel(part, index, grad_pre, w_self, returned, *refs):
    out, held, total, sems = refs[-4:]
    size = held.shape[0] // sems.shape[0]
    copies = copies_of(returned, held, size, sems)
    for copy in copies:
        copy.start()
    turned = lax.dot_general(
        w_self[part * WIDTH : (part + 1) * WIDTH, :],
        grad_pre[...],
        (((1,), (1,)), ((), ())),
        preferred_element_type=F32,
    )
    for t in range(4):
        total[t] = turned[:, t * 128 : (t + 1) * 128]
    for i, copy in enumerate(copies):
        copy.wait()
        for j in range(i * size, (i + 1) * size):
            total[index[j]] += held[j].astype(F32)
    for t in range(4):
        out[t] = total[t].T.astype(BF16)


def place(part, index, grad_pre, w_self, returned, earlier=None):
    def whole(shape):
        return pl.BlockSpec(shape, lambda *_: (0,) * len(shape))

    return pl.pallas_call(
        functools.partial(place_kernel, part),
        out_shape=jax.ShapeDtypeStruct((4, 128, 256), BF16),
        grid_spec=pltpu.PrefetchScalarGridSpec(
            num_scalar_prefetch=1,
            grid=(1,),
            in_specs=[whole(grad_pre.shape), whole(w_self.shape), pl.BlockSpec(memory_space=pl.ANY)]
            + ([] if earlier is None else [pl.BlockSpec(memory_space=pl.ANY)]),
            out_specs=pl.BlockSpec((4, 128, WIDTH), lambda *_: (0, 0, part)),
            scratch_shapes=[
                pltpu.VMEM((32, WIDTH, 128), BF16),
                pltpu.VMEM((4, WIDTH, 128), F32),
                pltpu.SemaphoreType.DMA((8,)),
            ],
        ),
        input_output_aliases={} if earlier is None else {4: 0},
        compiler_params=pltpu.CompilerParams(vmem_limit_bytes=8 * 2**20),
        name="place",
    )(index, grad_pre, w_self, returned, *([] if earlier is None else [earlier]))


def assemble_kernel(returned, w_self, w_neigh, held, sem):
    rows = returned.shape[1] - WIDTH
    copy = pltpu.make_async_copy(returned.at[:, pl.ds(WIDTH, rows)], held, sem)
    copy.start()
    copy.wait()
    scale = 1.0 / math.sqrt(512 * 256)
    for i in range(16):
        for out, block in ((w_self, held[i]), (w_neigh, held[16 + i])):
            block = block.astype(F32) * scale
            out[i, :, :128] = block[:16]
            out[i, :, 128:] = block[16:]


def assemble(returned):
    half = jax.ShapeDtypeStruct((16, 16, 256), F32)
    w_self, w_neigh = pl.pallas_call(
        assemble_kernel,
        out_shape=[half, half],
        in_specs=[pl.BlockSpec(memory_space=pl.ANY)],
        scratch_shapes=[pltpu.VMEM((32, 32, 128), BF16), pltpu.SemaphoreType.DMA],
        compiler_params=pltpu.CompilerParams(vmem_limit_bytes=8 * 2**20),
        name="assemble",
    )(returned)
    return w_self.reshape(256, 256), w_neigh.reshape(256, 256)


def sum_over_rep(share):
    share = share + flip(share, "c", 1)
    share = share + flip(share, "x", 1)
    return share + flip(share, "x", 2)


def shift(a, axis, by):
    size = lax.axis_size(axis)
    return lax.ppermute(a, axis, [(i, (i + by) % size) for i in range(size)])


def flip(a, axis, bit):
    return lax.ppermute(a, axis, [(i, i ^ bit) for i in range(lax.axis_size(axis))])


def body(
    features, cotangent, w_self, w_neigh, tile_values, tile_rows, tile_sources, tile_counts, needed
):
    z, y, x, c = (lax.axis_index(a) for a in AXES)
    rank = x * 2 + c
    values = tile_values[0, 0]
    rows = tile_rows[0, 0]
    sources = tile_sources[0, 0]
    info = jnp.stack([tile_counts[0, 0], x.astype(jnp.int32), c.astype(jnp.int32)])
    inside = jnp.arange(rows.shape[0]) < tile_counts[0, 0]
    forward_targets = jnp.where(inside, rows, 32)
    backward_targets = jnp.where(inside, sources, 32)
    backward_places = jnp.where((rows // 4) % 2 == c, 0, 16) + ((x - rows // 8) & 3) * 4 + rows % 4

    with jax.named_scope("gather_columns"):
        asked = lax.dynamic_slice(needed, (0, rank, z * 4 + y), (32, 1, 1)).reshape(32)
        outgoing = select(asked, features.reshape(4, 128, 256))
        columns = lax.all_to_all(outgoing, DOM, 0, 0, tiled=True)

    with jax.named_scope("aggregate"):
        shapes = [(4, 4, 128, 256)] * 2
        kept, sent = over_slots(
            forward_kernel, "forward", shapes, forward_targets, sources, info, values, [columns]
        )
        other = shift(sent, "c", 1)
        sums = []
        for k in range(4):
            pair = (kept[k].astype(F32) + other[k].astype(F32)).astype(BF16)
            sums.append((shift(pair, "x", k) if k else pair).reshape(512, 256))

    with jax.named_scope("dense"):
        output, grad_pre, *grad_aggs, local_weights = dense(features, cotangent, w_self, w_neigh, sums)

    with jax.named_scope("backward"):
        returned = []
        for h, part in enumerate(grad_aggs):
            behind = [part] + [shift(part, "x", k) for k in (1, 2, 3)]
            pieces, extra = list(behind), []
            if h == 0:
                local_weights, *pieces[:4] = lax.optimization_barrier((local_weights, *pieces[:4]))
                local_weights = lax.all_to_all(
                    local_weights.reshape(32, 16, 256), DOM, 0, 0, tiled=True
                )
            pieces += [shift(piece, "c", 1) for piece in pieces]
            if h == 1:
                share = sum_over_rep(local_weights.astype(F32).sum(0)).astype(BF16)
                extra = [jnp.concatenate([share[:, :128], share[:, 128:]])]
            (neighbour,) = over_slots(
                backward_kernel,
                "backward",
                [(32, WIDTH + 32 * len(extra), 128)],
                backward_targets,
                backward_places,
                info,
                values,
                pieces,
                extra,
            )
            returned.append(lax.all_to_all(neighbour, DOM, 0, 0, tiled=True))

    with jax.named_scope("weights"):
        grad_w_self, grad_w_neigh = assemble(returned[1])

    with jax.named_scope("final"):
        grad_features = None
        for h in range(PARTS):
            grad_features = place(h, asked, grad_pre, w_self, returned[h], grad_features)

    return (output, grad_features.reshape(512, 256), grad_w_self, grad_w_neigh)


def solution(mesh):
    chips = Mesh(mesh.devices.reshape(SIZES), AXES)
    nodes = P(AXES, None)
    in_specs = (
        nodes,
        nodes,
        P(),
        P(),
        P(DOM, REP, None, None, None),
        P(DOM, REP, None),
        P(DOM, REP, None),
        P(DOM, REP),
        P(),
    )
    out_specs = (nodes, nodes, P(), P())
    return jax.shard_map(body, mesh=chips, in_specs=in_specs, out_specs=out_specs, check_vma=False)
```

```python
import functools
import math

import jax
import jax.numpy as jnp
from jax import lax
from jax.experimental import pallas as pl
from jax.experimental.pallas import tpu as pltpu
from jax.sharding import Mesh
from jax.sharding import PartitionSpec as P

F32 = jnp.float32
BF16 = jnp.bfloat16
PARTS = 2
WIDTH = 256 // PARTS
BLOCK = 16
GROUP = 32
AHEAD = 8
VMEM_LIMIT = 48 * 2**20
AXES = ("z", "y", "x", "c")
SIZES = (8, 4, 4, 2)
DOM = ("z", "y")
REP = ("x", "c")


def select_kernel(index, blocks, out):
    for i in range(out.shape[0]):
        out[i] = blocks[index[i]]


def select(index, blocks):
    return pl.pallas_call(
        select_kernel,
        out_shape=jax.ShapeDtypeStruct((index.shape[0],) + blocks.shape[1:], blocks.dtype),
        grid_spec=pltpu.PrefetchScalarGridSpec(
            num_scalar_prefetch=1,
            grid=(),
            in_specs=[pl.BlockSpec(memory_space=pltpu.VMEM)],
            out_specs=pl.BlockSpec(memory_space=pltpu.VMEM),
        ),
        compiler_params=pltpu.CompilerParams(vmem_limit_bytes=8 * 2**20),
        name="select",
    )(index, blocks)


def copies_of(source, target, size, sems):
    rows = pl.ds(0, target.shape[1])
    return [
        pltpu.make_async_copy(
            source.at[pl.ds(i * size, size), rows], target.at[pl.ds(i * size, size)], sems.at[i]
        )
        for i in range(source.shape[0] // size)
    ]


def accumulate_slots(used, values, tiles, total, sems, piece_copies, add_slot):
    blocks = values.shape[0] // BLOCK

    def copy_of(b):
        span = pl.ds(b * BLOCK, BLOCK)
        return pltpu.make_async_copy(values.at[span], tiles.at[span], sems.at[b])

    for copy in piece_copies:
        copy.start()
    for b in range(AHEAD):
        copy_of(b).start()
    total[...] = jnp.zeros_like(total)
    for copy in piece_copies:
        copy.wait()

    def group(g, carry):
        for i in range(GROUP // BLOCK):
            b = g * (GROUP // BLOCK) + i
            copy_of(b).wait()

            @pl.when(b + AHEAD < blocks)
            def _():
                copy_of(b + AHEAD).start()

        @pl.when(g * GROUP < used)
        def _():
            for u in range(GROUP):
                add_slot(g * GROUP + u)

        return carry

    lax.fori_loop(0, values.shape[0] // GROUP, group, 0)


def forward_kernel(targets, places, info, values, columns, keep, send, tiles, total, sems):
    used, x, core = info[0], info[1], info[2]

    def add_slot(k):
        total[targets[k]] += jnp.dot(tiles[k], columns[places[k]], preferred_element_type=F32)

    accumulate_slots(used, values, tiles, total, sems, [], add_slot)
    for k in range(4):
        chip = lax.rem(x + k, 4) * 8
        keep[k] = total[pl.ds(chip + core * 4, 4)].astype(BF16)
        send[k] = total[pl.ds(chip + (1 - core) * 4, 4)].astype(BF16)


def backward_kernel(targets, places, info, values, *refs):
    pieces, (out, tiles, total, sems, held, piece_sems, rounded) = refs[:8], refs[-7:]

    def add_slot(k):
        total[targets[k]] += jnp.dot(held[places[k]], tiles[k], preferred_element_type=F32)

    piece_copies = [
        pltpu.make_async_copy(piece, held.at[pl.ds(i * 4, 4)], piece_sems.at[i])
        for i, piece in enumerate(pieces)
    ]
    accumulate_slots(info[0], values, tiles, total, sems, piece_copies, add_slot)
    copies = copies_of(rounded, out, 4, piece_sems)
    for i, copy in enumerate(copies):
        span = slice(4 * i, 4 * i + 4)
        rounded[span, :WIDTH, :] = total[span].astype(BF16)
        for share in refs[8:-7]:
            for j in range(4 * i, 4 * i + 4):
                rounded[j, WIDTH:, :] = share[...]
        copy.start()
    for copy in copies:
        copy.wait()


def over_slots(kernel, name, out_shapes, targets, places, info, values, pieces, extra=()):
    slots = values.shape[0]
    tile = pieces[0].shape[1:]
    scratch = [
        pltpu.VMEM(values.shape, BF16),
        pltpu.VMEM((33,) + tile, F32),
        pltpu.SemaphoreType.DMA((slots // BLOCK,)),
    ]
    if len(pieces) > 1:
        scratch += [
            pltpu.VMEM((32,) + tile, BF16),
            pltpu.SemaphoreType.DMA((len(pieces),)),
            pltpu.VMEM(out_shapes[0], BF16),
        ]
    piece_space = pl.ANY if len(pieces) > 1 else pltpu.VMEM
    return pl.pallas_call(
        kernel,
        out_shape=[jax.ShapeDtypeStruct(shape, BF16) for shape in out_shapes],
        grid_spec=pltpu.PrefetchScalarGridSpec(
            num_scalar_prefetch=3,
            grid=(),
            in_specs=[pl.BlockSpec(memory_space=pltpu.HBM)]
            + [pl.BlockSpec(memory_space=piece_space)] * len(pieces)
            + [pl.BlockSpec(memory_space=pltpu.VMEM)] * len(extra),
            out_specs=[pl.BlockSpec(memory_space=piece_space)] * len(out_shapes),
            scratch_shapes=scratch,
        ),
        compiler_params=pltpu.CompilerParams(vmem_limit_bytes=VMEM_LIMIT),
        cost_estimate=pl.CostEstimate(
            flops=2 * slots * 128 * 128 * 256, bytes_accessed=slots * 32768 + 2**22, transcendentals=0
        ),
        name=name,
    )(targets, places, info, values, *pieces, *extra)


def dense_kernel(features, cotangent, w_self, w_neigh, *refs):
    sums, refs = refs[:4], refs[4:]
    output, grad_pre, grad_aggs, local_weights = refs[0], refs[1], refs[2 : 2 + PARTS], refs[2 + PARTS]
    summed = sums[0][...].astype(F32)
    for part in sums[1:]:
        summed += part[...].astype(F32)
    agg = summed.astype(BF16)
    pre = jnp.dot(features[...], w_self[...], preferred_element_type=F32)
    pre += jnp.dot(agg, w_neigh[...], preferred_element_type=F32)
    logistic = jax.nn.sigmoid(pre)
    output[...] = (pre * logistic).astype(BF16)
    derivative = logistic * (1.0 + pre * (1.0 - logistic))
    grad = (cotangent[...].astype(F32) * derivative).astype(BF16)
    grad_pre[...] = grad
    for h in range(PARTS):
        turned = lax.dot_general(
            w_neigh[h * WIDTH : (h + 1) * WIDTH, :],
            grad,
            (((1,), (1,)), ((), ())),
            preferred_element_type=F32,
        ).astype(BF16)
        for t in range(4):
            grad_aggs[h][t] = turned[:, t * 128 : (t + 1) * 128]
    for i, left in enumerate((features[...], agg)):
        product = lax.dot_general(left, grad, (((0,), (0,)), ((), ())), preferred_element_type=F32)
        local_weights[i * 256 : (i + 1) * 256, :] = product.astype(BF16)


def dense(features, cotangent, w_self, w_neigh, sums):
    whole = jax.ShapeDtypeStruct(features.shape, BF16)
    part = jax.ShapeDtypeStruct((4, WIDTH, 128), BF16)
    return pl.pallas_call(
        dense_kernel,
        out_shape=[whole, whole] + [part] * PARTS + [whole],
        compiler_params=pltpu.CompilerParams(vmem_limit_bytes=16 * 2**20),
        name="dense",
    )(features, cotangent, w_self, w_neigh, *sums)


def place_kernel(part, index, grad_pre, w_self, returned, *refs):
    out, held, total, sems = refs[-4:]
    size = held.shape[0] // sems.shape[0]
    copies = copies_of(returned, held, size, sems)
    for copy in copies:
        copy.start()
    turned = lax.dot_general(
        w_self[part * WIDTH : (part + 1) * WIDTH, :],
        grad_pre[...],
        (((1,), (1,)), ((), ())),
        preferred_element_type=F32,
    )
    for t in range(4):
        total[t] = turned[:, t * 128 : (t + 1) * 128]
    for i, copy in enumerate(copies):
        copy.wait()
        for j in range(i * size, (i + 1) * size):
            total[index[j]] += held[j].astype(F32)
    for t in range(4):
        out[t] = total[t].T.astype(BF16)


def place(part, index, grad_pre, w_self, returned, earlier=None):
    def whole(shape):
        return pl.BlockSpec(shape, lambda *_: (0,) * len(shape))

    return pl.pallas_call(
        functools.partial(place_kernel, part),
        out_shape=jax.ShapeDtypeStruct((4, 128, 256), BF16),
        grid_spec=pltpu.PrefetchScalarGridSpec(
            num_scalar_prefetch=1,
            grid=(1,),
            in_specs=[whole(grad_pre.shape), whole(w_self.shape), pl.BlockSpec(memory_space=pl.ANY)]
            + ([] if earlier is None else [pl.BlockSpec(memory_space=pl.ANY)]),
            out_specs=pl.BlockSpec((4, 128, WIDTH), lambda *_: (0, 0, part)),
            scratch_shapes=[
                pltpu.VMEM((32, WIDTH, 128), BF16),
                pltpu.VMEM((4, WIDTH, 128), F32),
                pltpu.SemaphoreType.DMA((8,)),
            ],
        ),
        input_output_aliases={} if earlier is None else {4: 0},
        compiler_params=pltpu.CompilerParams(vmem_limit_bytes=8 * 2**20),
        name="place",
    )(index, grad_pre, w_self, returned, *([] if earlier is None else [earlier]))


def assemble_kernel(returned, w_self, w_neigh, held, sem):
    rows = returned.shape[1] - WIDTH
    copy = pltpu.make_async_copy(returned.at[:, pl.ds(WIDTH, rows)], held, sem)
    copy.start()
    copy.wait()
    scale = 1.0 / math.sqrt(512 * 256)
    for i in range(16):
        for out, block in ((w_self, held[i]), (w_neigh, held[16 + i])):
            block = block.astype(F32) * scale
            out[i, :, :128] = block[:16]
            out[i, :, 128:] = block[16:]


def assemble(returned):
    half = jax.ShapeDtypeStruct((16, 16, 256), F32)
    w_self, w_neigh = pl.pallas_call(
        assemble_kernel,
        out_shape=[half, half],
        in_specs=[pl.BlockSpec(memory_space=pl.ANY)],
        scratch_shapes=[pltpu.VMEM((32, 32, 128), BF16), pltpu.SemaphoreType.DMA],
        compiler_params=pltpu.CompilerParams(vmem_limit_bytes=8 * 2**20),
        name="assemble",
    )(returned)
    return w_self.reshape(256, 256), w_neigh.reshape(256, 256)


def sum_over_rep(share):
    share = share + flip(share, "c", 1)
    share = share + flip(share, "x", 1)
    return share + flip(share, "x", 2)


def shift(a, axis, by):
    size = lax.axis_size(axis)
    return lax.ppermute(a, axis, [(i, (i + by) % size) for i in range(size)])


def flip(a, axis, bit):
    return lax.ppermute(a, axis, [(i, i ^ bit) for i in range(lax.axis_size(axis))])


def body(
    features, cotangent, w_self, w_neigh, tile_values, tile_rows, tile_sources, tile_counts, needed
):
    z, y, x, c = (lax.axis_index(a) for a in AXES)
    rank = x * 2 + c
    values = tile_values[0, 0]
    rows = tile_rows[0, 0]
    sources = tile_sources[0, 0]
    info = jnp.stack([tile_counts[0, 0], x.astype(jnp.int32), c.astype(jnp.int32)])
    inside = jnp.arange(rows.shape[0]) < tile_counts[0, 0]
    forward_targets = jnp.where(inside, rows, 32)
    backward_targets = jnp.where(inside, sources, 32)
    backward_places = jnp.where((rows // 4) % 2 == c, 0, 16) + ((x - rows // 8) & 3) * 4 + rows % 4

    with jax.named_scope("gather_columns"):
        asked = lax.dynamic_slice(needed, (0, rank, z * 4 + y), (32, 1, 1)).reshape(32)
        outgoing = select(asked, features.reshape(4, 128, 256))
        columns = lax.all_to_all(outgoing, DOM, 0, 0, tiled=True)

    with jax.named_scope("aggregate"):
        shapes = [(4, 4, 128, 256)] * 2
        kept, sent = over_slots(
            forward_kernel, "forward", shapes, forward_targets, sources, info, values, [columns]
        )
        other = shift(sent, "c", 1)
        sums = []
        for k in range(4):
            pair = (kept[k].astype(F32) + other[k].astype(F32)).astype(BF16)
            sums.append((shift(pair, "x", k) if k else pair).reshape(512, 256))

    with jax.named_scope("dense"):
        output, grad_pre, *grad_aggs, local_weights = dense(features, cotangent, w_self, w_neigh, sums)

    with jax.named_scope("backward"):
        returned = []
        for h, part in enumerate(grad_aggs):
            behind = [part, shift(part, "x", 1), None, shift(part, "x", 3)]
            behind[2] = shift(behind[1], "x", 1)
            pieces, extra = list(behind), []
            if h == 0:
                local_weights, pieces[1], pieces[3] = lax.optimization_barrier(
                    (local_weights, pieces[1], pieces[3])
                )
                local_weights = lax.all_to_all(
                    local_weights.reshape(32, 16, 256), DOM, 0, 0, tiled=True
                )
            pieces += [shift(piece, "c", 1) for piece in pieces]
            if h == 1:
                share = sum_over_rep(local_weights.astype(F32).sum(0)).astype(BF16)
                extra = [jnp.concatenate([share[:, :128], share[:, 128:]])]
            (neighbour,) = over_slots(
                backward_kernel,
                "backward",
                [(32, WIDTH + 32 * len(extra), 128)],
                backward_targets,
                backward_places,
                info,
                values,
                pieces,
                extra,
            )
            returned.append(lax.all_to_all(neighbour, DOM, 0, 0, tiled=True))

    with jax.named_scope("weights"):
        grad_w_self, grad_w_neigh = assemble(returned[1])

    with jax.named_scope("final"):
        grad_features = None
        for h in range(PARTS):
            grad_features = place(h, asked, grad_pre, w_self, returned[h], grad_features)

    return (output, grad_features.reshape(512, 256), grad_w_self, grad_w_neigh)


def solution(mesh):
    chips = Mesh(mesh.devices.reshape(SIZES), AXES)
    nodes = P(AXES, None)
    in_specs = (
        nodes,
        nodes,
        P(),
        P(),
        P(DOM, REP, None, None, None),
        P(DOM, REP, None),
        P(DOM, REP, None),
        P(DOM, REP),
        P(),
    )
    out_specs = (nodes, nodes, P(), P())
    return jax.shard_map(body, mesh=chips, in_specs=in_specs, out_specs=out_specs, check_vma=False)
```

```python
import functools
import math

import jax
import jax.numpy as jnp
from jax import lax
from jax.experimental import pallas as pl
from jax.experimental.pallas import tpu as pltpu
from jax.sharding import Mesh
from jax.sharding import PartitionSpec as P

F32 = jnp.float32
BF16 = jnp.bfloat16
PARTS = 2
WIDTH = 256 // PARTS
BLOCK = 16
GROUP = 32
AHEAD = 8
VMEM_LIMIT = 48 * 2**20
AXES = ("z", "y", "x", "c")
SIZES = (8, 4, 4, 2)
DOM = ("z", "y")
REP = ("x", "c")


def select_kernel(index, blocks, out):
    for i in range(out.shape[0]):
        out[i] = blocks[index[i]]


def select(index, blocks):
    return pl.pallas_call(
        select_kernel,
        out_shape=jax.ShapeDtypeStruct((index.shape[0],) + blocks.shape[1:], blocks.dtype),
        grid_spec=pltpu.PrefetchScalarGridSpec(
            num_scalar_prefetch=1,
            grid=(),
            in_specs=[pl.BlockSpec(memory_space=pltpu.VMEM)],
            out_specs=pl.BlockSpec(memory_space=pltpu.VMEM),
        ),
        compiler_params=pltpu.CompilerParams(vmem_limit_bytes=8 * 2**20),
        name="select",
    )(index, blocks)


def copies_of(source, target, size, sems):
    rows = pl.ds(0, target.shape[1])
    return [
        pltpu.make_async_copy(
            source.at[pl.ds(i * size, size), rows], target.at[pl.ds(i * size, size)], sems.at[i]
        )
        for i in range(source.shape[0] // size)
    ]


def accumulate_slots(used, values, tiles, total, sems, piece_copies, add_slot):
    blocks = values.shape[0] // BLOCK

    def copy_of(b):
        span = pl.ds(b * BLOCK, BLOCK)
        return pltpu.make_async_copy(values.at[span], tiles.at[span], sems.at[b])

    for copy in piece_copies:
        copy.start()
    for b in range(AHEAD):
        copy_of(b).start()
    total[...] = jnp.zeros_like(total)
    for copy in piece_copies:
        copy.wait()

    def group(g, carry):
        for i in range(GROUP // BLOCK):
            b = g * (GROUP // BLOCK) + i
            copy_of(b).wait()

            @pl.when(b + AHEAD < blocks)
            def _():
                copy_of(b + AHEAD).start()

        @pl.when(g * GROUP < used)
        def _():
            for u in range(GROUP):
                add_slot(g * GROUP + u)

        return carry

    lax.fori_loop(0, values.shape[0] // GROUP, group, 0)


def forward_kernel(targets, places, info, values, columns, keep, send, tiles, total, sems):
    used, x, core = info[0], info[1], info[2]

    def add_slot(k):
        total[targets[k]] += jnp.dot(tiles[k], columns[places[k]], preferred_element_type=F32)

    accumulate_slots(used, values, tiles, total, sems, [], add_slot)
    for k in range(4):
        chip = lax.rem(x + k, 4) * 8
        keep[k] = total[pl.ds(chip + core * 4, 4)].astype(BF16)
        send[k] = total[pl.ds(chip + (1 - core) * 4, 4)].astype(BF16)


def backward_kernel(targets, places, info, values, *refs):
    pieces, (out, tiles, total, sems, held, piece_sems, rounded) = refs[:8], refs[-7:]

    def add_slot(k):
        total[targets[k]] += jnp.dot(held[places[k]], tiles[k], preferred_element_type=F32)

    piece_copies = [
        pltpu.make_async_copy(piece, held.at[pl.ds(i * 4, 4)], piece_sems.at[i])
        for i, piece in enumerate(pieces)
    ]
    accumulate_slots(info[0], values, tiles, total, sems, piece_copies, add_slot)
    copies = copies_of(rounded, out, 4, piece_sems)
    for i, copy in enumerate(copies):
        span = slice(4 * i, 4 * i + 4)
        rounded[span, :WIDTH, :] = total[span].astype(BF16)
        for share in refs[8:-7]:
            for j in range(4 * i, 4 * i + 4):
                rounded[j, WIDTH:, :] = share[...]
        copy.start()
    for copy in copies:
        copy.wait()


def over_slots(kernel, name, out_shapes, targets, places, info, values, pieces, extra=()):
    slots = values.shape[0]
    tile = pieces[0].shape[1:]
    scratch = [
        pltpu.VMEM(values.shape, BF16),
        pltpu.VMEM((33,) + tile, F32),
        pltpu.SemaphoreType.DMA((slots // BLOCK,)),
    ]
    if len(pieces) > 1:
        scratch += [
            pltpu.VMEM((32,) + tile, BF16),
            pltpu.SemaphoreType.DMA((len(pieces),)),
            pltpu.VMEM(out_shapes[0], BF16),
        ]
    piece_space = pl.ANY if len(pieces) > 1 else pltpu.VMEM
    return pl.pallas_call(
        kernel,
        out_shape=[jax.ShapeDtypeStruct(shape, BF16) for shape in out_shapes],
        grid_spec=pltpu.PrefetchScalarGridSpec(
            num_scalar_prefetch=3,
            grid=(),
            in_specs=[pl.BlockSpec(memory_space=pltpu.HBM)]
            + [pl.BlockSpec(memory_space=piece_space)] * len(pieces)
            + [pl.BlockSpec(memory_space=pltpu.VMEM)] * len(extra),
            out_specs=[pl.BlockSpec(memory_space=piece_space)] * len(out_shapes),
            scratch_shapes=scratch,
        ),
        compiler_params=pltpu.CompilerParams(vmem_limit_bytes=VMEM_LIMIT),
        cost_estimate=pl.CostEstimate(
            flops=2 * slots * 128 * 128 * 256, bytes_accessed=slots * 32768 + 2**22, transcendentals=0
        ),
        name=name,
    )(targets, places, info, values, *pieces, *extra)


def dense_kernel(features, cotangent, w_self, w_neigh, *refs):
    sums, refs = refs[:4], refs[4:]
    output, grad_pre, grad_aggs, local_weights = refs[0], refs[1], refs[2 : 2 + PARTS], refs[2 + PARTS]
    summed = sums[0][...].astype(F32)
    for part in sums[1:]:
        summed += part[...].astype(F32)
    agg = summed.astype(BF16)
    pre = jnp.dot(features[...], w_self[...], preferred_element_type=F32)
    pre += jnp.dot(agg, w_neigh[...], preferred_element_type=F32)
    logistic = jax.nn.sigmoid(pre)
    output[...] = (pre * logistic).astype(BF16)
    derivative = logistic * (1.0 + pre * (1.0 - logistic))
    grad = (cotangent[...].astype(F32) * derivative).astype(BF16)
    grad_pre[...] = grad
    for h in range(PARTS):
        turned = lax.dot_general(
            w_neigh[h * WIDTH : (h + 1) * WIDTH, :],
            grad,
            (((1,), (1,)), ((), ())),
            preferred_element_type=F32,
        ).astype(BF16)
        for t in range(4):
            grad_aggs[h][t] = turned[:, t * 128 : (t + 1) * 128]
    for i, left in enumerate((features[...], agg)):
        product = lax.dot_general(left, grad, (((0,), (0,)), ((), ())), preferred_element_type=F32)
        local_weights[i * 256 : (i + 1) * 256, :] = product.astype(BF16)


def dense(features, cotangent, w_self, w_neigh, sums):
    whole = jax.ShapeDtypeStruct(features.shape, BF16)
    part = jax.ShapeDtypeStruct((4, WIDTH, 128), BF16)
    return pl.pallas_call(
        dense_kernel,
        out_shape=[whole, whole] + [part] * PARTS + [whole],
        compiler_params=pltpu.CompilerParams(vmem_limit_bytes=16 * 2**20),
        name="dense",
    )(features, cotangent, w_self, w_neigh, *sums)


def place_kernel(part, index, grad_pre, w_self, returned, *refs):
    out, held, total, sems = refs[-4:]
    size = held.shape[0] // sems.shape[0]
    copies = copies_of(returned, held, size, sems)
    for copy in copies:
        copy.start()
    turned = lax.dot_general(
        w_self[part * WIDTH : (part + 1) * WIDTH, :],
        grad_pre[...],
        (((1,), (1,)), ((), ())),
        preferred_element_type=F32,
    )
    for t in range(4):
        total[t] = turned[:, t * 128 : (t + 1) * 128]
    for i, copy in enumerate(copies):
        copy.wait()
        for j in range(i * size, (i + 1) * size):
            total[index[j]] += held[j].astype(F32)
    for t in range(4):
        out[t] = total[t].T.astype(BF16)


def place(part, index, grad_pre, w_self, returned, earlier=None):
    def whole(shape):
        return pl.BlockSpec(shape, lambda *_: (0,) * len(shape))

    return pl.pallas_call(
        functools.partial(place_kernel, part),
        out_shape=jax.ShapeDtypeStruct((4, 128, 256), BF16),
        grid_spec=pltpu.PrefetchScalarGridSpec(
            num_scalar_prefetch=1,
            grid=(1,),
            in_specs=[whole(grad_pre.shape), whole(w_self.shape), pl.BlockSpec(memory_space=pl.ANY)]
            + ([] if earlier is None else [pl.BlockSpec(memory_space=pl.ANY)]),
            out_specs=pl.BlockSpec((4, 128, WIDTH), lambda *_: (0, 0, part)),
            scratch_shapes=[
                pltpu.VMEM((32, WIDTH, 128), BF16),
                pltpu.VMEM((4, WIDTH, 128), F32),
                pltpu.SemaphoreType.DMA((8,)),
            ],
        ),
        input_output_aliases={} if earlier is None else {4: 0},
        compiler_params=pltpu.CompilerParams(vmem_limit_bytes=8 * 2**20),
        name="place",
    )(index, grad_pre, w_self, returned, *([] if earlier is None else [earlier]))


def assemble_kernel(info, own, other, w_self, w_neigh):
    core = info[0]
    scale = 1.0 / math.sqrt(512 * 256)
    for i in range(32):
        out = (w_self, w_neigh)[i // 16]
        for piece, at in ((own, core), (other, 1 - core)):
            block = piece[i].astype(F32) * scale
            rows = pl.ds(at * 8, 8)
            out[i % 16, rows, :128] = block[:8]
            out[i % 16, rows, 128:] = block[8:]


def assemble(rows):
    half = jax.ShapeDtypeStruct((16, 16, 256), F32)
    w_self, w_neigh = pl.pallas_call(
        assemble_kernel,
        out_shape=[half, half],
        grid_spec=pltpu.PrefetchScalarGridSpec(
            num_scalar_prefetch=1,
            grid=(),
            in_specs=[pl.BlockSpec(memory_space=pltpu.VMEM)] * 2,
            out_specs=[pl.BlockSpec(memory_space=pltpu.VMEM)] * 2,
        ),
        compiler_params=pltpu.CompilerParams(vmem_limit_bytes=8 * 2**20),
        name="assemble",
    )(lax.axis_index("c").astype(jnp.int32)[None], rows, shift(rows, "c", 1))
    return w_self.reshape(256, 256), w_neigh.reshape(256, 256)


def sum_over_rep(share):
    c = lax.axis_index("c")
    own, other = (lax.dynamic_slice(share, (i * 8, 0), (8, 256)) for i in (c, 1 - c))
    share = own + shift(other, "c", 1)
    share = share + flip(share, "x", 1)
    return share + flip(share, "x", 2)


def shift(a, axis, by):
    size = lax.axis_size(axis)
    return lax.ppermute(a, axis, [(i, (i + by) % size) for i in range(size)])


def flip(a, axis, bit):
    return lax.ppermute(a, axis, [(i, i ^ bit) for i in range(lax.axis_size(axis))])


def body(
    features, cotangent, w_self, w_neigh, tile_values, tile_rows, tile_sources, tile_counts, needed
):
    z, y, x, c = (lax.axis_index(a) for a in AXES)
    rank = x * 2 + c
    values = tile_values[0, 0]
    rows = tile_rows[0, 0]
    sources = tile_sources[0, 0]
    info = jnp.stack([tile_counts[0, 0], x.astype(jnp.int32), c.astype(jnp.int32)])
    inside = jnp.arange(rows.shape[0]) < tile_counts[0, 0]
    forward_targets = jnp.where(inside, rows, 32)
    backward_targets = jnp.where(inside, sources, 32)
    backward_places = jnp.where((rows // 4) % 2 == c, 0, 16) + ((x - rows // 8) & 3) * 4 + rows % 4

    with jax.named_scope("gather_columns"):
        asked = lax.dynamic_slice(needed, (0, rank, z * 4 + y), (32, 1, 1)).reshape(32)
        outgoing = select(asked, features.reshape(4, 128, 256))
        columns = lax.all_to_all(outgoing, DOM, 0, 0, tiled=True)

    with jax.named_scope("aggregate"):
        shapes = [(4, 4, 128, 256)] * 2
        kept, sent = over_slots(
            forward_kernel, "forward", shapes, forward_targets, sources, info, values, [columns]
        )
        other = shift(sent, "c", 1)
        sums = []
        for k in range(4):
            pair = (kept[k].astype(F32) + other[k].astype(F32)).astype(BF16)
            sums.append((shift(pair, "x", k) if k else pair).reshape(512, 256))

    with jax.named_scope("dense"):
        output, grad_pre, *grad_aggs, local_weights = dense(features, cotangent, w_self, w_neigh, sums)

    with jax.named_scope("backward"):
        returned = []
        for h, part in enumerate(grad_aggs):
            behind = [part, shift(part, "x", 1), None, shift(part, "x", 3)]
            behind[2] = shift(behind[1], "x", 1)
            pieces, extra = list(behind), []
            if h == 0:
                local_weights, pieces[1], pieces[3] = lax.optimization_barrier(
                    (local_weights, pieces[1], pieces[3])
                )
                local_weights = lax.all_to_all(
                    local_weights.reshape(32, 16, 256), DOM, 0, 0, tiled=True
                )
            pieces += [shift(piece, "c", 1) for piece in pieces]
            if h == 1:
                share = sum_over_rep(local_weights.astype(F32).sum(0)).astype(BF16)
                extra = [jnp.concatenate([share[:, :128], share[:, 128:]])]
            (neighbour,) = over_slots(
                backward_kernel,
                "backward",
                [(32, WIDTH + 16 * len(extra), 128)],
                backward_targets,
                backward_places,
                info,
                values,
                pieces,
                extra,
            )
            if h == 1:
                neighbour, returned[0] = lax.optimization_barrier((neighbour, returned[0]))
            returned.append(lax.all_to_all(neighbour, DOM, 0, 0, tiled=True))

    with jax.named_scope("final"):
        grad_features = place(0, asked, grad_pre, w_self, returned[0])
        weight_rows = returned[1][:, WIDTH:, :]
        weight_rows, grad_features = lax.optimization_barrier((weight_rows, grad_features))
        grad_features = place(1, asked, grad_pre, w_self, returned[1], grad_features)

    with jax.named_scope("weights"):
        grad_w_self, grad_w_neigh = assemble(weight_rows)

    return (output, grad_features.reshape(512, 256), grad_w_self, grad_w_neigh)


def solution(mesh):
    chips = Mesh(mesh.devices.reshape(SIZES), AXES)
    nodes = P(AXES, None)
    in_specs = (
        nodes,
        nodes,
        P(),
        P(),
        P(DOM, REP, None, None, None),
        P(DOM, REP, None),
        P(DOM, REP, None),
        P(DOM, REP),
        P(),
    )
    out_specs = (nodes, nodes, P(), P())
    return jax.shard_map(body, mesh=chips, in_specs=in_specs, out_specs=out_specs, check_vma=False)
```

```python
import functools
import math

import jax
import jax.numpy as jnp
from jax import lax
from jax.experimental import pallas as pl
from jax.experimental.pallas import tpu as pltpu
from jax.sharding import Mesh
from jax.sharding import PartitionSpec as P

F32 = jnp.float32
BF16 = jnp.bfloat16
PARTS = 2
WIDTH = 256 // PARTS
BLOCK = 16
GROUP = 32
AHEAD = 8
VMEM_LIMIT = 48 * 2**20
AXES = ("z", "y", "x", "c")
SIZES = (8, 4, 4, 2)
DOM = ("z", "y")
REP = ("x", "c")


def select_kernel(index, *refs):
    blocks, out = refs[:-1], refs[-1]
    for i in range(out.shape[0]):
        out[i] = blocks[i % len(blocks)][index[i]]


def select(index, blocks):
    shape = (index.shape[0],) + blocks[0].shape[1:]
    return pl.pallas_call(
        select_kernel,
        out_shape=jax.ShapeDtypeStruct(shape, blocks[0].dtype),
        grid_spec=pltpu.PrefetchScalarGridSpec(
            num_scalar_prefetch=1,
            grid=(),
            in_specs=[pl.BlockSpec(memory_space=pltpu.VMEM)] * len(blocks),
            out_specs=pl.BlockSpec(memory_space=pltpu.VMEM),
        ),
        compiler_params=pltpu.CompilerParams(vmem_limit_bytes=8 * 2**20),
        name="select",
    )(index, *blocks)


def copies_of(source, target, size, sems):
    rows = pl.ds(0, target.shape[1])
    return [
        pltpu.make_async_copy(
            source.at[pl.ds(i * size, size), rows], target.at[pl.ds(i * size, size)], sems.at[i]
        )
        for i in range(source.shape[0] // size)
    ]


def accumulate_slots(used, values, tiles, total, sems, piece_copies, add_slot):
    blocks = values.shape[0] // BLOCK

    def copy_of(b):
        span = pl.ds(b * BLOCK, BLOCK)
        return pltpu.make_async_copy(values.at[span], tiles.at[span], sems.at[b])

    for copy in piece_copies:
        copy.start()
    for b in range(AHEAD):
        copy_of(b).start()
    total[...] = jnp.zeros_like(total)
    for copy in piece_copies:
        copy.wait()

    def group(g, carry):
        for i in range(GROUP // BLOCK):
            b = g * (GROUP // BLOCK) + i
            copy_of(b).wait()

            @pl.when(b + AHEAD < blocks)
            def _():
                copy_of(b + AHEAD).start()

        @pl.when(g * GROUP < used)
        def _():
            for u in range(GROUP):
                add_slot(g * GROUP + u)

        return carry

    lax.fori_loop(0, values.shape[0] // GROUP, group, 0)


def forward_kernel(targets, places, info, values, first, second, keep, send, *scratch):
    tiles, total, sems, held, piece_sems = scratch
    used, x, core = info[0], info[1], info[2]

    def add_slot(k):
        total[targets[k]] += jnp.dot(tiles[k], held[places[k]], preferred_element_type=F32)

    piece_copies = [
        pltpu.make_async_copy(piece, held.at[pl.ds(i * 16, 16)], piece_sems.at[i])
        for i, piece in enumerate((first, second))
    ]
    accumulate_slots(used, values, tiles, total, sems, piece_copies, add_slot)
    for k in range(4):
        chip = lax.rem(x + k, 4) * 8
        keep[k] = total[pl.ds(chip + core * 4, 4)].astype(BF16)
        send[k] = total[pl.ds(chip + (1 - core) * 4, 4)].astype(BF16)


def backward_kernel(targets, places, info, values, *refs):
    pieces, (out, tiles, total, sems, held, piece_sems, rounded) = refs[:8], refs[-7:]

    def add_slot(k):
        total[targets[k]] += jnp.dot(held[places[k]], tiles[k], preferred_element_type=F32)

    piece_copies = [
        pltpu.make_async_copy(piece, held.at[pl.ds(i * 4, 4)], piece_sems.at[i])
        for i, piece in enumerate(pieces)
    ]
    accumulate_slots(info[0], values, tiles, total, sems, piece_copies, add_slot)
    copies = copies_of(rounded, out, 4, piece_sems)
    for i, copy in enumerate(copies):
        span = slice(4 * i, 4 * i + 4)
        rounded[span, :WIDTH, :] = total[span].astype(BF16)
        for share in refs[8:-7]:
            for j in range(4 * i, 4 * i + 4):
                rounded[j, WIDTH:, :] = share[...]
        copy.start()
    for copy in copies:
        copy.wait()


def over_slots(kernel, name, out_shapes, targets, places, info, values, pieces, extra=()):
    slots = values.shape[0]
    tile = pieces[0].shape[1:]
    scratch = [
        pltpu.VMEM(values.shape, BF16),
        pltpu.VMEM((33,) + tile, F32),
        pltpu.SemaphoreType.DMA((slots // BLOCK,)),
    ]
    scratch += [pltpu.VMEM((32,) + tile, BF16), pltpu.SemaphoreType.DMA((len(pieces),))]
    if len(out_shapes) == 1:
        scratch.append(pltpu.VMEM(out_shapes[0], BF16))
    out_space = pl.ANY if len(out_shapes) == 1 else pltpu.VMEM
    return pl.pallas_call(
        kernel,
        out_shape=[jax.ShapeDtypeStruct(shape, BF16) for shape in out_shapes],
        grid_spec=pltpu.PrefetchScalarGridSpec(
            num_scalar_prefetch=3,
            grid=(),
            in_specs=[pl.BlockSpec(memory_space=pltpu.HBM)]
            + [pl.BlockSpec(memory_space=pl.ANY)] * len(pieces)
            + [pl.BlockSpec(memory_space=pltpu.VMEM)] * len(extra),
            out_specs=[pl.BlockSpec(memory_space=out_space)] * len(out_shapes),
            scratch_shapes=scratch,
        ),
        compiler_params=pltpu.CompilerParams(vmem_limit_bytes=VMEM_LIMIT),
        cost_estimate=pl.CostEstimate(
            flops=2 * slots * 128 * 128 * 256, bytes_accessed=slots * 32768 + 2**22, transcendentals=0
        ),
        name=name,
    )(targets, places, info, values, *pieces, *extra)


def dense_kernel(features, cotangent, w_self, w_neigh, *refs):
    sums, refs = refs[:4], refs[4:]
    output, grad_pre, grad_aggs, local_weights = refs[0], refs[1], refs[2 : 2 + PARTS], refs[2 + PARTS]
    summed = sums[0][...].astype(F32)
    for part in sums[1:]:
        summed += part[...].astype(F32)
    agg = summed.astype(BF16)
    pre = jnp.dot(features[...], w_self[...], preferred_element_type=F32)
    pre += jnp.dot(agg, w_neigh[...], preferred_element_type=F32)
    logistic = jax.nn.sigmoid(pre)
    output[...] = (pre * logistic).astype(BF16)
    derivative = logistic * (1.0 + pre * (1.0 - logistic))
    grad = (cotangent[...].astype(F32) * derivative).astype(BF16)
    grad_pre[...] = grad
    for h in range(PARTS):
        turned = lax.dot_general(
            w_neigh[h * WIDTH : (h + 1) * WIDTH, :],
            grad,
            (((1,), (1,)), ((), ())),
            preferred_element_type=F32,
        ).astype(BF16)
        for t in range(4):
            grad_aggs[h][t] = turned[:, t * 128 : (t + 1) * 128]
    for i, left in enumerate((features[...], agg)):
        product = lax.dot_general(left, grad, (((0,), (0,)), ((), ())), preferred_element_type=F32)
        local_weights[i * 256 : (i + 1) * 256, :] = product.astype(BF16)


def dense(features, cotangent, w_self, w_neigh, sums):
    whole = jax.ShapeDtypeStruct(features.shape, BF16)
    part = jax.ShapeDtypeStruct((4, WIDTH, 128), BF16)
    return pl.pallas_call(
        dense_kernel,
        out_shape=[whole, whole] + [part] * PARTS + [whole],
        compiler_params=pltpu.CompilerParams(vmem_limit_bytes=16 * 2**20),
        name="dense",
    )(features, cotangent, w_self, w_neigh, *sums)


def place_kernel(part, index, grad_pre, w_self, returned, *refs):
    out, held, total, sems = refs[-4:]
    size = held.shape[0] // sems.shape[0]
    copies = copies_of(returned, held, size, sems)
    for copy in copies:
        copy.start()
    turned = lax.dot_general(
        w_self[part * WIDTH : (part + 1) * WIDTH, :],
        grad_pre[...],
        (((1,), (1,)), ((), ())),
        preferred_element_type=F32,
    )
    for t in range(4):
        total[t] = turned[:, t * 128 : (t + 1) * 128]
    for i, copy in enumerate(copies):
        copy.wait()
        for j in range(i * size, (i + 1) * size):
            total[index[j]] += held[j].astype(F32)
    for t in range(4):
        out[t] = total[t].T.astype(BF16)


def place(part, index, grad_pre, w_self, returned, earlier=None):
    def whole(shape):
        return pl.BlockSpec(shape, lambda *_: (0,) * len(shape))

    return pl.pallas_call(
        functools.partial(place_kernel, part),
        out_shape=jax.ShapeDtypeStruct((4, 128, 256), BF16),
        grid_spec=pltpu.PrefetchScalarGridSpec(
            num_scalar_prefetch=1,
            grid=(1,),
            in_specs=[whole(grad_pre.shape), whole(w_self.shape), pl.BlockSpec(memory_space=pl.ANY)]
            + ([] if earlier is None else [pl.BlockSpec(memory_space=pl.ANY)]),
            out_specs=pl.BlockSpec((4, 128, WIDTH), lambda *_: (0, 0, part)),
            scratch_shapes=[
                pltpu.VMEM((32, WIDTH, 128), BF16),
                pltpu.VMEM((4, WIDTH, 128), F32),
                pltpu.SemaphoreType.DMA((8,)),
            ],
        ),
        input_output_aliases={} if earlier is None else {4: 0},
        compiler_params=pltpu.CompilerParams(vmem_limit_bytes=8 * 2**20),
        name="place",
    )(index, grad_pre, w_self, returned, *([] if earlier is None else [earlier]))


def assemble_kernel(info, own, other, w_self, w_neigh):
    core = info[0]
    scale = 1.0 / math.sqrt(512 * 256)
    for i in range(32):
        out = (w_self, w_neigh)[i // 16]
        for piece, at in ((own, core), (other, 1 - core)):
            block = piece[i].astype(F32) * scale
            rows = pl.ds(at * 8, 8)
            out[i % 16, rows, :128] = block[:8]
            out[i % 16, rows, 128:] = block[8:]


def assemble(rows):
    half = jax.ShapeDtypeStruct((16, 16, 256), F32)
    w_self, w_neigh = pl.pallas_call(
        assemble_kernel,
        out_shape=[half, half],
        grid_spec=pltpu.PrefetchScalarGridSpec(
            num_scalar_prefetch=1,
            grid=(),
            in_specs=[pl.BlockSpec(memory_space=pltpu.VMEM)] * 2,
            out_specs=[pl.BlockSpec(memory_space=pltpu.VMEM)] * 2,
        ),
        compiler_params=pltpu.CompilerParams(vmem_limit_bytes=8 * 2**20),
        name="assemble",
    )(lax.axis_index("c").astype(jnp.int32)[None], rows, shift(rows, "c", 1))
    return w_self.reshape(256, 256), w_neigh.reshape(256, 256)


def sum_over_rep(share):
    c = lax.axis_index("c")
    own, other = (lax.dynamic_slice(share, (i * 8, 0), (8, 256)) for i in (c, 1 - c))
    share = own + shift(other, "c", 1)
    share = share + flip(share, "x", 1)
    return share + flip(share, "x", 2)


def shift(a, axis, by):
    size = lax.axis_size(axis)
    return lax.ppermute(a, axis, [(i, (i + by) % size) for i in range(size)])


def flip(a, axis, bit):
    return lax.ppermute(a, axis, [(i, i ^ bit) for i in range(lax.axis_size(axis))])


def body(
    features, cotangent, w_self, w_neigh, tile_values, tile_rows, tile_sources, tile_counts, needed
):
    z, y, x, c = (lax.axis_index(a) for a in AXES)
    rank = x * 2 + c
    values = tile_values[0, 0]
    rows = tile_rows[0, 0]
    sources = tile_sources[0, 0]
    info = jnp.stack([tile_counts[0, 0], x.astype(jnp.int32), c.astype(jnp.int32)])
    inside = jnp.arange(rows.shape[0]) < tile_counts[0, 0]
    forward_targets = jnp.where(inside, rows, 32)
    backward_targets = jnp.where(inside, sources, 32)
    backward_places = jnp.where((rows // 4) % 2 == c, 0, 16) + ((x - rows // 8) & 3) * 4 + rows % 4

    with jax.named_scope("gather_columns"):
        asked = lax.dynamic_slice(needed, (0, rank, z * 4 + y), (32, 1, 1)).reshape(32)
        wanted = lax.dynamic_slice(
            needed.reshape(8, 4, 8, 8, 4), (z, 0, rank, 0, y), (1, 4, 1, 8, 1)
        ).reshape(4, 8)
        blocks = {0: features.reshape(4, 128, 256)}
        for k in (1, 2, 3, 4):
            blocks[k] = shift(blocks[k - 1], "z", 1)
            if k < 4:
                blocks[8 - k] = shift(blocks[(9 - k) % 8], "z", 7)
        columns = []
        for group in ((0, 1, 7, 2), (6, 3, 5, 4)):
            index = jnp.stack([wanted[:, (z - k) % 8] for k in group], 1).reshape(16)
            outgoing = select(index, [blocks[k] for k in group])
            if not columns:
                asked, outgoing = lax.optimization_barrier((asked, outgoing))
            columns.append(lax.all_to_all(outgoing, "y", 0, 0, tiled=True))
        order = jnp.array([0, 1, 3, 5, 7, 6, 4, 2], jnp.int32)[(z - sources // 4) % 8]
        forward_places = order // 4 * 16 + sources % 4 * 4 + order % 4

    with jax.named_scope("aggregate"):
        shapes = [(4, 4, 128, 256)] * 2
        kept, sent = over_slots(
            forward_kernel, "forward", shapes, forward_targets, forward_places, info, values, columns
        )
        other = shift(sent, "c", 1)
        sums = []
        for k in range(4):
            pair = (kept[k].astype(F32) + other[k].astype(F32)).astype(BF16)
            sums.append((shift(pair, "x", k) if k else pair).reshape(512, 256))

    with jax.named_scope("dense"):
        output, grad_pre, *grad_aggs, local_weights = dense(features, cotangent, w_self, w_neigh, sums)

    with jax.named_scope("backward"):
        returned = []
        for h, part in enumerate(grad_aggs):
            behind = [part, shift(part, "x", 1), None, shift(part, "x", 3)]
            behind[2] = shift(behind[1], "x", 1)
            pieces, extra = list(behind), []
            if h == 0:
                local_weights, pieces[1], pieces[3] = lax.optimization_barrier(
                    (local_weights, pieces[1], pieces[3])
                )
                local_weights = lax.all_to_all(
                    local_weights.reshape(32, 16, 256), DOM, 0, 0, tiled=True
                )
            pieces += [shift(piece, "c", 1) for piece in pieces]
            if h == 1:
                share = sum_over_rep(local_weights.astype(F32).sum(0)).astype(BF16)
                extra = [jnp.concatenate([share[:, :128], share[:, 128:]])]
            (neighbour,) = over_slots(
                backward_kernel,
                "backward",
                [(32, WIDTH + 16 * len(extra), 128)],
                backward_targets,
                backward_places,
                info,
                values,
                pieces,
                extra,
            )
            if h == 1:
                neighbour, returned[0] = lax.optimization_barrier((neighbour, returned[0]))
            returned.append(lax.all_to_all(neighbour, DOM, 0, 0, tiled=True))

    with jax.named_scope("final"):
        grad_features = place(0, asked, grad_pre, w_self, returned[0])
        weight_rows = returned[1][:, WIDTH:, :]
        weight_rows, grad_features = lax.optimization_barrier((weight_rows, grad_features))
        grad_features = place(1, asked, grad_pre, w_self, returned[1], grad_features)

    with jax.named_scope("weights"):
        grad_w_self, grad_w_neigh = assemble(weight_rows)

    return (output, grad_features.reshape(512, 256), grad_w_self, grad_w_neigh)


def solution(mesh):
    chips = Mesh(mesh.devices.reshape(SIZES), AXES)
    nodes = P(AXES, None)
    in_specs = (
        nodes,
        nodes,
        P(),
        P(),
        P(DOM, REP, None, None, None),
        P(DOM, REP, None),
        P(DOM, REP, None),
        P(DOM, REP),
        P(),
    )
    out_specs = (nodes, nodes, P(), P())
    return jax.shard_map(body, mesh=chips, in_specs=in_specs, out_specs=out_specs, check_vma=False)
```
